32 devices in a mesh: dp: 8 (over z, x), section: 4 (over y, core).
Axes of the slice: x: 2, y: 2, z: 4, core: 2. Of those that a mesh axis runs over, the one named last changes fastest.
Arguments:
- tap_maps: bfloat16 [4, 2, 1024, 3200], P(None, None, ('dp', 'section')), may hold values from -6 to 6
- lateral_weight: bfloat16 [4, 3200, 768], P('section', 'dp'), may hold values from -0.109375 to 0.109375
- conv_weight: bfloat16 [4, 6912, 768], P('section'), may hold values from -0.078125 to 0.078125
- classifier: bfloat16 [768, 150], replicated, may hold values from -0.875 to 0.875
- tile_counts: int32 [8, 2], P('dp'), may hold values from 1 to 2, as said below
- labels: int32 [2, 1024], P(None, 'dp'), may hold values from 0 to 149
Outputs:
- conv_grad: float32 [4, 6912, 768], P('section', 'dp')
- lateral_grad: float32 [4, 3200, 768], P('section', 'dp')
The draws below stay inside these ranges and needn't reach their ends.
Inputs may be any that keep to these rules, and one draw needn't show every extreme that they name: `tile_counts`: some entry equals 2.
All inputs are finite; a program needn't handle non-finite values.
Results may differ from the reference program's by a relative error of at most 0.035.
Values may be sent and summed in bfloat16 or wider, within the bound.
No kernel may reach another device: no remote copies, remote signals or barrier semaphores. Data moves between devices by JAX's collectives and lax.ppermute only.
A program may use at most 128 MiB of HBM per device.

```python
import jax
import jax.numpy as jnp
from jax import lax

WIDTH = 3200
CHANNELS = 768
CLASSES = 150
TAPS = 4
MICRO = 2
TILE_CAP = 2
BAND_ROWS = 1
BAND_COLS = 64
PIXELS = 128
ALL_PIXELS = 1024
N_DP = 8
N_SECTION = 4


def draw_tile_counts(key, part):
    first_key, second_key = jax.random.split(key)
    counts = jax.random.randint(first_key, (N_DP * MICRO,), 1, TILE_CAP + 1)
    target = jax.random.randint(second_key, (), 0, N_DP * MICRO)
    counts = jnp.where(jnp.arange(N_DP * MICRO) == target, TILE_CAP, counts)
    return counts.reshape(N_DP, MICRO).astype(jnp.int32)


def plant(drawn, own_key, low, largest):
    longest = drawn.shape.index(max(drawn.shape))
    spots = []
    for shift in (0, 1):
        where = [jax.random.randint(jax.random.fold_in(own_key, axis), (), 0, length) for axis, length in enumerate(drawn.shape)]
        where[longest] = (where[longest] + shift) % drawn.shape[longest]
        spots.append(tuple(where))
    return drawn.at[spots[0]].set(low).at[spots[1]].set(largest)


def block_levels(key, shape, shards, least, largest):
    def one(dim, shards_of):
        heights = jax.random.uniform(jax.random.fold_in(jax.random.fold_in(key, 6), dim), (shards_of,), jnp.float32, least / len(shards), largest / len(shards))
        return jnp.repeat(jnp.exp(heights), shape[dim] // shards_of).reshape((-1,) + (1,) * (len(shape) - dim - 1))

    level = one(*shards[0])
    for cut in shards[1:]:
        level = level * one(*cut)
    return level


def noise(rng, dims, deviation, most, shards=(), kind=jnp.bfloat16):
    gain = block_levels(rng, dims, shards, -0.22, 0.18) if shards else 1.0
    values = jax.random.normal(rng, dims, jnp.float32) * deviation * gain
    return jnp.minimum(jnp.maximum(values, -most), most).astype(kind)


def setup_inputs(seed: int = 0) -> dict:
    streams_of = jax.random.split(jax.random.key(seed), 7)
    tap_maps = noise(streams_of[0], (TAPS, MICRO, ALL_PIXELS, WIDTH), 1.0, 6.0, ((2, 32),))
    lateral_weight = noise(streams_of[1], (N_SECTION, WIDTH, CHANNELS), WIDTH ** -0.5, 0.109375, ((0, 4), (1, 8)))
    conv_weight = noise(streams_of[2], (N_SECTION, 9 * CHANNELS, CHANNELS), (9 * CHANNELS) ** -0.5, 0.078125, ((0, 4),))
    classifier = noise(streams_of[3], (CHANNELS, CLASSES), (CHANNELS // 16) ** -0.5, 0.875)
    tile_counts = draw_tile_counts(jax.random.fold_in(streams_of[6], 71), 0)
    labels = plant(jax.random.randint(streams_of[5], (MICRO, ALL_PIXELS), 0, CLASSES), jax.random.fold_in(streams_of[5], 1), 0, CLASSES - 1).astype(jnp.int32)
    return {"tap_maps": tap_maps, "lateral_weight": lateral_weight, "conv_weight": conv_weight, "classifier": classifier, "tile_counts": tile_counts, "labels": labels}


def neighbour_shifts():
    return [(row_shift, col_shift) for row_shift in (-1, 0, 1) for col_shift in (-1, 0, 1)]


def to_tiles(field):
    micros = field.shape[0]
    chans = field.shape[-1]
    grid = field.reshape(micros, N_DP, TILE_CAP, BAND_ROWS, BAND_COLS, chans).transpose(0, 2, 1, 3, 4, 5)
    return grid.reshape(micros * TILE_CAP, N_DP * BAND_ROWS, BAND_COLS, chans)


def from_tiles(grid, micros):
    chans = grid.shape[-1]
    parts = grid.reshape(micros, TILE_CAP, N_DP, BAND_ROWS, BAND_COLS, chans).transpose(0, 2, 1, 3, 4, 5)
    return parts.reshape(micros, N_DP * PIXELS, chans)


def to_columns(field):
    micros = field.shape[0]
    grid = to_tiles(field)
    rows = grid.shape[1]
    padded = jnp.pad(grid, ((0, 0), (1, 1), (1, 1), (0, 0)))
    pieces = [padded[:, 1 + rs:1 + rs + rows, 1 + cs:1 + cs + BAND_COLS, :] for rs, cs in neighbour_shifts()]
    return from_tiles(jnp.concatenate(pieces, axis=-1), micros)


def from_columns(grads):
    micros = grads.shape[0]
    chans = grads.shape[-1] // 9
    grid = to_tiles(grads)
    rows = grid.shape[1]
    grid = grid.reshape(grid.shape[0], rows, BAND_COLS, 9, chans)
    total = jnp.zeros((grid.shape[0], rows + 2, BAND_COLS + 2, chans), jnp.float32)
    for offset, (rs, cs) in enumerate(neighbour_shifts()):
        total = total + jnp.pad(grid[:, :, :, offset, :].astype(jnp.float32), ((0, 0), (1 + rs, 1 - rs), (1 + cs, 1 - cs), (0, 0)))
    return from_tiles(total[:, 1:-1, 1:-1, :], micros)


def group_partials(left, right):
    depth = left.shape[-1]
    lefts = left.reshape(MICRO, N_DP, PIXELS, depth).transpose(1, 0, 2, 3).reshape(N_DP, MICRO * PIXELS, depth)
    rights = right.reshape(MICRO, N_DP, PIXELS, CHANNELS).transpose(1, 0, 2, 3).reshape(N_DP, MICRO * PIXELS, CHANNELS)

    def one_group(pair):
        return jnp.dot(pair[0].T, pair[1], preferred_element_type=jnp.float32).astype(jnp.bfloat16)

    rounded = lax.map(one_group, (lefts, rights))
    rounded = lax.optimization_barrier(rounded)
    return jnp.sum(rounded.astype(jnp.float32), axis=0)


def reference(tap_maps, lateral_weight, conv_weight, classifier, tile_counts, labels):
    band = BAND_ROWS * BAND_COLS
    npix = labels.shape[1]
    position = jnp.arange(npix)
    group = position // PIXELS
    slot = (position % PIXELS) // band
    per_count = tile_counts.T[:, group]
    valid = (slot[None, :] < per_count).astype(jnp.float32)
    pixel_weight = valid / (per_count.astype(jnp.float32) * band * N_DP * MICRO)
    activated = jnp.zeros((MICRO, npix, CHANNELS), jnp.bfloat16)
    summed_list = []
    preact_list = []
    for section in range(N_SECTION):
        level = section * TAPS // N_SECTION
        lateral = jnp.dot(tap_maps[level].reshape(-1, WIDTH), lateral_weight[section], preferred_element_type=jnp.float32).reshape(MICRO, npix, CHANNELS)
        summed = (activated.astype(jnp.float32) + lateral).astype(jnp.bfloat16)
        columns = to_columns(summed)
        preact = jnp.dot(columns.reshape(-1, 9 * CHANNELS), conv_weight[section], preferred_element_type=jnp.float32).reshape(MICRO, npix, CHANNELS)
        activated = jax.nn.silu(preact).astype(jnp.bfloat16)
        summed_list.append(summed)
        preact_list.append(preact)
    logits = jnp.dot(activated.reshape(-1, CHANNELS), classifier, preferred_element_type=jnp.float32).reshape(MICRO, npix, CLASSES)
    expo = jnp.exp(logits)
    probs = expo / jnp.sum(expo, axis=-1, keepdims=True)
    onehot = (labels[:, :, None] == jnp.arange(CLASSES)[None, None, :]).astype(jnp.float32)
    grad_logits = ((probs - onehot) * pixel_weight[:, :, None]).astype(jnp.bfloat16)
    grad_out = jnp.dot(grad_logits.reshape(-1, CLASSES), classifier.T, preferred_element_type=jnp.float32).reshape(MICRO, npix, CHANNELS)
    conv_grads = [None] * N_SECTION
    lateral_grads = [None] * N_SECTION
    for section in range(N_SECTION - 1, -1, -1):
        level = section * TAPS // N_SECTION
        preact = preact_list[section]
        sigma = jax.nn.sigmoid(preact)
        grad_pre = (grad_out * sigma * (1.0 + preact * (1.0 - sigma))).astype(jnp.bfloat16)
        columns = to_columns(summed_list[section])
        conv_grads[section] = group_partials(columns, grad_pre)
        grad_cols = jnp.dot(grad_pre.reshape(-1, CHANNELS), conv_weight[section].T, preferred_element_type=jnp.float32).reshape(MICRO, npix, 9 * CHANNELS)
        grad_in = from_columns(grad_cols).astype(jnp.bfloat16)
        lateral_grads[section] = group_partials(tap_maps[level], grad_in)
        grad_out = grad_in.astype(jnp.float32)
    return jnp.stack(conv_grads), jnp.stack(lateral_grads)
```

```python
import functools

import jax
import jax.numpy as jnp
from jax import lax
from jax.experimental import pallas as pl
from jax.experimental.pallas import tpu as pltpu
from jax.sharding import PartitionSpec as P

TILE_CAP = 2
BAND_ROWS = 1
BAND_COLS = 64
VMEM_LIMIT = 60 * 1024 * 1024


def neighbour_shifts():
    return [(row_shift, col_shift) for row_shift in (-1, 0, 1) for col_shift in (-1, 0, 1)]


def ring_order(groups):
    return list(range(0, groups, 2)) + list(range(1, groups, 2))[::-1]


def ring_gather(block, use, state):
    groups = lax.axis_size("dp")
    order = ring_order(groups)
    up_route = [(order[i], order[(i + 1) % groups]) for i in range(groups)]
    down_route = [(j, i) for i, j in up_route]
    table = jnp.array(order, jnp.int32)
    spot = position_of(order)
    state = use(state, lax.axis_index("dp"), block)
    up = down = block
    for step in range(1, groups // 2):
        up = lax.ppermute(up, "dp", up_route)
        down = lax.ppermute(down, "dp", down_route)
        state = use(state, table[(spot - step) % groups], up)
        state = use(state, table[(spot + step) % groups], down)
    half = block.shape[0] // 2
    first = lax.ppermute(up[:half], "dp", up_route)
    second = lax.ppermute(down[half:], "dp", down_route)
    return use(state, table[(spot + groups // 2) % groups], jnp.concatenate([first, second]))


def position_of(order):
    places = [0] * len(order)
    for place, device in enumerate(order):
        places[device] = place
    return jnp.array(places, jnp.int32)[lax.axis_index("dp")]


def put(buffer, index, block):
    return lax.dynamic_update_index_in_dim(buffer, block, index, 0)


def write_shifts(value, rows, cols, pads_ref):
    count = rows * cols
    col = lax.broadcasted_iota(jnp.int32, value.shape, 0) % cols
    zeros = jnp.zeros((cols, value.shape[1]), jnp.float32)
    left = jnp.where(col == 0, 0.0, pltpu.roll(value, 1, 0))
    right = jnp.where(col == cols - 1, 0.0, pltpu.roll(value, count - 1, 0))
    for j, moved in enumerate((left, value, right)):
        pads_ref[j, 0:cols, :] = zeros
        pads_ref[j, cols : cols + count, :] = moved
        pads_ref[j, cols + count : count + 2 * cols, :] = zeros


def forward_kernel(rows, cols, active_ref, x_ref, lateral_ref, w_ref, out_ref, summed_ref, preact_ref, pads_ref):
    chans = x_ref.shape[1]
    count = rows * cols

    @pl.when(active_ref[0] > 0)
    def _():
        summed = (x_ref[...].astype(jnp.float32) + lateral_ref[...].astype(jnp.float32)).astype(jnp.bfloat16)
        summed_ref[...] = summed
        write_shifts(summed.astype(jnp.float32), rows, cols, pads_ref)
        total = jnp.zeros((count, chans), jnp.float32)
        for offset, (dr, dc) in enumerate(neighbour_shifts()):
            lhs = pads_ref[dc + 1, (1 + dr) * cols : (1 + dr) * cols + count, :].astype(jnp.bfloat16)
            total = total + jnp.dot(lhs, w_ref[offset * chans : (offset + 1) * chans, :], preferred_element_type=jnp.float32)
        preact_ref[...] = total
        out_ref[...] = (total / (1.0 + jnp.exp(-total))).astype(jnp.bfloat16)


def backward_kernel(
    rows, cols, classes, has_loss, active_ref, in_ref, preact_ref, w_ref, *refs
):
    if has_loss:
        classifier_ref, labels_ref, weight_ref, pre_ref, out_ref, pads_ref = refs
    else:
        pre_ref, out_ref, pads_ref = refs
    chans = preact_ref.shape[1]
    count = rows * cols

    @pl.when(active_ref[0] > 0)
    def _():
        preact = preact_ref[...]
        if has_loss:
            logits = jnp.dot(in_ref[...], classifier_ref[...], preferred_element_type=jnp.float32)
            ids = lax.broadcasted_iota(jnp.int32, logits.shape, 1)
            expo = jnp.where(ids < classes, jnp.exp(logits), 0.0)
            probs = expo / jnp.sum(expo, axis=-1, keepdims=True)
            onehot = (labels_ref[...] == ids).astype(jnp.float32)
            grad_logits = ((probs - onehot) * weight_ref[...]).astype(jnp.bfloat16)
            grad_out = lax.dot_general(
                grad_logits, classifier_ref[...], (((1,), (1,)), ((), ())), preferred_element_type=jnp.float32
            )
        else:
            grad_out = in_ref[...].astype(jnp.float32)
        sigma = 1.0 / (1.0 + jnp.exp(-preact))
        grad_pre = (grad_out * sigma * (1.0 + preact * (1.0 - sigma))).astype(jnp.bfloat16)
        pre_ref[...] = grad_pre
        write_shifts(grad_pre.astype(jnp.float32), rows, cols, pads_ref)
        total = jnp.zeros((count, chans), jnp.float32)
        for offset, (dr, dc) in enumerate(neighbour_shifts()):
            lhs = pads_ref[1 - dc, (1 - dr) * cols : (1 - dr) * cols + count, :].astype(jnp.bfloat16)
            total = total + lax.dot_general(
                lhs,
                w_ref[offset * chans : (offset + 1) * chans, :],
                (((1,), (1,)), ((), ())),
                preferred_element_type=jnp.float32,
            )
        out_ref[...] = total.astype(jnp.bfloat16)


def on_device(tap_maps, lateral_weight, conv_weight, classifier, tile_counts, labels):
    sections = lax.axis_size("section")
    groups = lax.axis_size("dp")
    place = lax.axis_index("section")
    group = lax.axis_index("dp")
    levels, micros, local, width = tap_maps.shape
    pixels = labels.shape[1]
    chans = conv_weight.shape[2]
    classes = classifier.shape[1]
    tiles = micros * TILE_CAP
    rows = groups * BAND_ROWS
    strips = groups // tiles
    own_cols = BAND_COLS // strips
    reach = -(-2 * sections // 8) * 8
    if strips == 1:
        cols = own_cols
    elif strips == 2:
        cols = own_cols + reach
    else:
        cols = min(BAND_COLS, own_cols + 2 * reach)
    starts = [min(max(h * own_cols - reach, 0), BAND_COLS - cols) for h in range(strips)]
    strip = group % strips
    own_start = jnp.array([h * own_cols - starts[h] for h in range(strips)], jnp.int32)[strip]
    count = rows * cols
    weights = conv_weight[0]

    def windows(field):
        grid = field.reshape(tiles, BAND_ROWS, BAND_COLS, field.shape[-1])
        parts = [lax.slice_in_dim(grid, s, s + cols, axis=2) for s in starts]
        return jnp.stack(parts, axis=1).reshape(groups, BAND_ROWS, cols, field.shape[-1])

    chosen = tap_maps if sections == levels else tap_maps[jnp.array([s * levels // sections for s in range(sections)])]
    tap_rows = lax.all_to_all(chosen, "section", 0, 0, tiled=True)
    depth = width // groups
    tap_blocks = tap_rows.reshape(sections * micros * local, groups, depth).transpose(1, 0, 2)

    def add_product(total, index, block):
        left = lax.dynamic_index_in_dim(tap_blocks, index, 0, keepdims=False)
        return total + jnp.dot(left, block, preferred_element_type=jnp.float32)

    lateral = ring_gather(
        lateral_weight[0], add_product, jnp.zeros((sections * micros * local, chans), jnp.float32)
    )
    lateral = lateral.astype(jnp.bfloat16).reshape(sections, micros, local, chans).transpose(1, 0, 2, 3)
    lateral = windows(lateral.reshape(micros, pixels, chans))
    lateral = lax.all_to_all(lateral, "dp", 0, 0, tiled=True).reshape(count, chans)

    band = BAND_ROWS * BAND_COLS
    slot_ids = jnp.arange(pixels) // band
    counts = jnp.broadcast_to(tile_counts[0][:, None], (micros, pixels))
    valid = (slot_ids[None, :] < counts).astype(jnp.int32)
    marks = windows(jnp.stack([labels, counts, valid], axis=-1))
    marks = lax.all_to_all(marks, "dp", 0, 0, tiled=True).reshape(count, 3)
    window_labels = marks[:, 0:1]
    window_weight = marks[:, 2:3].astype(jnp.float32) / (
        marks[:, 1:2].astype(jnp.float32) * band * groups * micros
    )
    padded_classes = -(-classes // 128) * 128
    wide_classifier = jnp.pad(classifier, ((0, 0), (0, padded_classes - classes)))

    vmem = pl.BlockSpec(memory_space=pltpu.VMEM)
    smem = pl.BlockSpec(memory_space=pltpu.SMEM)
    params = pltpu.CompilerParams(vmem_limit_bytes=VMEM_LIMIT)
    pads = pltpu.VMEM((3, count + 2 * cols, chans), jnp.float32)
    half = jax.ShapeDtypeStruct((count, chans), jnp.bfloat16)
    full = jax.ShapeDtypeStruct((count, chans), jnp.float32)

    def flag(section):
        return (place == section).astype(jnp.int32).reshape(1)

    run_forward = pl.pallas_call(
        functools.partial(forward_kernel, rows, cols),
        out_shape=(half, half, full),
        in_specs=[smem, vmem, vmem, vmem],
        out_specs=(vmem, vmem, vmem),
        scratch_shapes=[pads],
        compiler_params=params,
    )

    def run_backward(has_loss, *operands):
        return pl.pallas_call(
            functools.partial(backward_kernel, rows, cols, classes, has_loss),
            out_shape=(half, half),
            in_specs=[smem] + [vmem] * (len(operands) - 1),
            out_specs=(vmem, vmem),
            scratch_shapes=[pads],
            compiler_params=params,
        )(*operands)

    carried = jnp.zeros((count, chans), jnp.bfloat16)
    summed_of, preact_of = [], []
    for section in range(sections):
        if section:
            carried = lax.ppermute(carried, "section", [(section - 1, section)])
        carried, summed, preact = run_forward(flag(section), carried, lateral, weights)
        summed_of.append(summed)
        preact_of.append(preact)

    pre_of, grad_of = [None] * sections, [None] * sections
    for section in range(sections - 1, -1, -1):
        if section == sections - 1:
            result = run_backward(
                True, flag(section), carried, preact_of[section], weights, wide_classifier, window_labels, window_weight
            )
        else:
            carried = lax.ppermute(carried, "section", [(section + 1, section)])
            result = run_backward(False, flag(section), carried, preact_of[section], weights)
        pre_of[section], grad_of[section] = result
        carried = result[1]

    def owned(per_section):
        grid = lax.select_n(place, *per_section).reshape(rows, cols, chans)
        return lax.dynamic_slice_in_dim(grid, own_start, own_cols, axis=1).reshape(rows * own_cols, chans)

    def gathered(block):
        return ring_gather(block, put, jnp.zeros((groups,) + block.shape, block.dtype))

    summed_all = gathered(owned(summed_of)).reshape(tiles, strips, rows, own_cols, chans)
    grid = summed_all.transpose(0, 2, 1, 3, 4).reshape(tiles, rows, BAND_COLS, chans)
    grid = jnp.pad(grid, ((0, 0), (1, 1), (1, 1), (0, 0)))
    share = 9 * chans // groups
    begin = group * share
    offset = begin // chans
    pieces = []
    for k in range(-(-share // chans) + 1):
        which = jnp.minimum(offset + k, 8)
        pieces.append(
            lax.dynamic_slice(grid, (0, which // 3, which % 3, 0), (tiles, rows, BAND_COLS, chans))
        )
    column_part = lax.dynamic_slice_in_dim(jnp.concatenate(pieces, axis=-1), begin - offset * chans, share, axis=3)
    column_part = column_part.reshape(tiles, rows, strips, own_cols, share).transpose(0, 2, 1, 3, 4)
    column_part = column_part.reshape(tiles * strips * rows * own_cols, share)

    order = ring_order(groups)
    spots = position_of(order)
    table = jnp.array(order, jnp.int32)
    tap_part = jnp.zeros(tap_blocks.shape, tap_blocks.dtype)
    tap_part = put(tap_part, group, lax.dynamic_index_in_dim(tap_blocks, group, 0, keepdims=False))
    for k in range(1, groups):
        route = [(order[i], order[(i + k) % groups]) for i in range(groups)]
        outgoing = lax.dynamic_index_in_dim(tap_blocks, table[(spots + k) % groups], 0, keepdims=False)
        tap_part = put(tap_part, table[(spots - k) % groups], lax.ppermute(outgoing, "dp", route))
    tap_part = tap_part.reshape(groups, sections, micros, local, depth).transpose(2, 1, 3, 0, 4)
    tap_part = tap_part.reshape(micros, TILE_CAP, BAND_ROWS, strips, own_cols, groups, depth)
    tap_part = tap_part.transpose(0, 1, 3, 5, 2, 4, 6).reshape(-1, depth)

    grads = gathered(jnp.stack([owned(pre_of), owned(grad_of)]))
    pre_all = grads[:, 0].reshape(-1, chans)
    grad_all = grads[:, 1].reshape(-1, chans)
    contract = (((0,), (0,)), ((), ()))
    conv_grad = lax.dot_general(column_part, pre_all, contract, preferred_element_type=jnp.float32)
    lateral_grad = lax.dot_general(tap_part, grad_all, contract, preferred_element_type=jnp.float32)
    return (conv_grad[None], lateral_grad[None])


def solution(mesh):
    placed = (
        P(None, None, ("dp", "section"), None),
        P("section", "dp", None),
        P("section", None, None),
        P(),
        P("dp", None),
        P(None, "dp"),
    )
    return jax.shard_map(
        on_device,
        mesh=mesh,
        in_specs=placed,
        out_specs=(P("section", "dp", None), P("section", "dp", None)),
        check_vma=False,
    )
```

```python
import functools

import jax
import jax.numpy as jnp
from jax import lax
from jax.experimental import pallas as pl
from jax.experimental.pallas import tpu as pltpu
from jax.sharding import PartitionSpec as P

TILE_CAP = 2
BAND_ROWS = 1
BAND_COLS = 64
MARKS = 128


def neighbour_shifts():
    return [(row_shift, col_shift) for row_shift in (-1, 0, 1) for col_shift in (-1, 0, 1)]


def ring_order(groups):
    return list(range(0, groups, 2)) + list(range(1, groups, 2))[::-1]


def by_device(per_place):
    groups = len(per_place)
    order = ring_order(groups)
    listed = [per_place[order.index(device)] for device in range(groups)]
    return lax.dynamic_index_in_dim(jnp.array(listed, jnp.int32), lax.axis_index("dp"), 0, keepdims=False)


class Ring:
    def __init__(self, block):
        groups = lax.axis_size("dp")
        order = ring_order(groups)
        self.steps = groups // 2
        self.up_route = [(order[i], order[(i + 1) % groups]) for i in range(groups)]
        self.down_route = [(j, i) for i, j in self.up_route]
        self.done = 0
        self.up = self.down = block
        self.blocks = [block]
        steps = [sign * step for step in range(1, self.steps) for sign in (-1, 1)]
        self.sources = by_device([[(spot + shift) % groups for shift in [0] + steps + [self.steps]] for spot in range(groups)])

    def after(self, other):
        self.up, self.down, other = lax.optimization_barrier((self.up, self.down, other))
        return other

    def step(self):
        self.done += 1
        if self.done < self.steps:
            self.up = lax.ppermute(self.up, "dp", self.up_route)
            self.down = lax.ppermute(self.down, "dp", self.down_route)
        elif self.done == self.steps:
            half = self.up.shape[-1] // 2
            self.up = lax.ppermute(self.up[..., :half], "dp", self.up_route)
            self.down = lax.ppermute(self.down[..., half:], "dp", self.down_route)
        else:
            return
        self.blocks += [self.up, self.down]

    def finish(self):
        while self.done < self.steps:
            self.step()


def lateral_kernel(sources_ref, taps_ref, *refs):
    *block_refs, out_ref, total_ref = refs
    groups = taps_ref.shape[0]
    half = out_ref.shape[1] // 2
    contract = (((0,), (0,)), ((), ()))

    def product(k, block_ref):
        return lax.dot_general(taps_ref[sources_ref[k]], block_ref[...], contract, preferred_element_type=jnp.float32)

    for k in range(groups - 1):
        total_ref[...] = product(k, block_refs[k]) if k == 0 else total_ref[...] + product(k, block_refs[k])
    for j, spot in enumerate((slice(0, half), slice(half, 2 * half))):
        out_ref[:, spot] = (total_ref[:, spot] + product(groups - 1, block_refs[groups - 1 + j])).astype(jnp.bfloat16)


def repeat(times, unrolled, body):
    if times <= unrolled:
        for i in range(times):
            body(i)
    else:
        lax.fori_loop(0, times, lambda i, _: body(i), None)


def assemble(rows, strips, sources_ref, block_refs, grid_ref):
    own_cols = grid_ref.shape[3]
    half = grid_ref.shape[4] // 2
    blank = jnp.zeros((grid_ref.shape[0],) + grid_ref.shape[2:], grid_ref.dtype)
    grid_ref[:, 0] = blank
    grid_ref[:, rows + 1] = blank
    for k, block_ref in enumerate(block_refs):
        source = sources_ref[min(k, sources_ref.shape[0] - 1)]
        span = slice(0, 2 * half)
        if block_ref.shape[2] == half:
            span = slice(0, half) if k == sources_ref.shape[0] - 1 else slice(half, 2 * half)

        def copy_row(row, block_ref=block_ref, source=source, span=span):
            grid_ref[source // strips, 1 + row, source % strips, :, span] = block_ref[row]

        repeat(rows, 8, copy_row)


def transposed_convolution(tile, first, chunk, grid_ref, w_ref, pads_ref):
    chans = grid_ref.shape[4]
    size = (chunk + 2) * BAND_COLS
    value = grid_ref[tile, pl.ds(first, chunk + 2)].reshape(size, chans).astype(jnp.float32)
    col = lax.broadcasted_iota(jnp.int32, value.shape, 0) % BAND_COLS
    pads_ref[0] = jnp.where(col == 0, 0.0, pltpu.roll(value, 1, 0)).astype(jnp.bfloat16)
    pads_ref[1] = value.astype(jnp.bfloat16)
    pads_ref[2] = jnp.where(col == BAND_COLS - 1, 0.0, pltpu.roll(value, size - 1, 0)).astype(jnp.bfloat16)
    total = jnp.zeros((chunk * BAND_COLS, chans), jnp.float32)
    for offset, (dr, dc) in enumerate(neighbour_shifts()):
        total = total + lax.dot_general(
            pads_ref[1 - dc, (1 - dr) * BAND_COLS : (1 - dr + chunk) * BAND_COLS, :],
            w_ref[offset * chans : (offset + 1) * chans, :],
            (((1,), (1,)), ((), ())),
            preferred_element_type=jnp.float32,
        )
    return total.astype(jnp.bfloat16).reshape(chunk, BAND_COLS, chans)


def columns_kernel(rows, strips, chunk, sources_ref, spot_ref, *refs):
    *block_refs, out_ref, grid_ref, pads_ref, wide_ref = refs
    tiles, _, share = out_ref.shape[:3]
    chans = grid_ref.shape[4]
    assemble(rows, strips, sources_ref, block_refs, grid_ref)
    size = (chunk + 2) * BAND_COLS
    chunks = rows // chunk

    def fill(i):
        tile, first = i // chunks, i % chunks * chunk
        value = grid_ref[tile, pl.ds(first, chunk + 2)].reshape(size, chans).astype(jnp.float32)
        col = lax.broadcasted_iota(jnp.int32, value.shape, 0) % BAND_COLS
        pads_ref[0] = jnp.where(col == 0, 0.0, pltpu.roll(value, 1, 0))
        pads_ref[1] = value
        pads_ref[2] = jnp.where(col == BAND_COLS - 1, 0.0, pltpu.roll(value, size - 1, 0))
        for piece in range(wide_ref.shape[0] // chans):
            offset = jnp.minimum(spot_ref[0] + piece, 8)
            at = pl.multiple_of(offset // 3 * BAND_COLS, BAND_COLS)
            moved = pads_ref[offset % 3, pl.ds(at, chunk * BAND_COLS), :]
            wide_ref[piece * chans : (piece + 1) * chans, :] = moved.T
        part = wide_ref[pl.ds(pl.multiple_of(spot_ref[1], 8), share), :]
        out_ref[tile, i % chunks] = part.astype(jnp.bfloat16)

    repeat(tiles * chunks, 4, fill)


def early_gradient_kernel(rows, strips, chunk, sources_ref, todo_ref, w_ref, *refs):
    *block_refs, inner_ref, grid_ref, pads_ref = refs
    assemble(rows, strips, sources_ref, block_refs, grid_ref)
    chunks = rows // chunk

    def convolve(i):
        first = i % chunks * chunk
        values = transposed_convolution(todo_ref[i // chunks], first, chunk, grid_ref, w_ref, pads_ref)
        inner_ref[i // chunks, pl.ds(first, chunk)] = values

    repeat(inner_ref.shape[0] * chunks, 4, convolve)


def late_gradient_kernel(
    rows, strips, chunk, sections, micros, sources_ref, todo_ref, group_ref, w_ref, columns_ref, inner_ref, *refs
):
    *other_refs, conv_ref, lateral_ref, grid_ref, pads_ref, all_ref, right_ref = refs
    tiles, groups = grid_ref.shape[0], sources_ref.shape[0]
    tap_refs, block_refs = other_refs[:groups], other_refs[groups:]
    chans = grid_ref.shape[4]
    assemble(rows, strips, sources_ref, block_refs, grid_ref)
    chunks = rows // chunk
    conv_ref[...] = jnp.zeros_like(conv_ref)

    def multiply(i):
        right = grid_ref[i // chunks, pl.ds(1 + i % chunks * chunk, chunk)].reshape(chunk * BAND_COLS, chans)
        conv_ref[...] += jnp.dot(columns_ref[i // chunks, i % chunks], right, preferred_element_type=jnp.float32)

    repeat(tiles * chunks, 4, multiply)
    known = inner_ref.shape[0]
    for j in range(known):
        all_ref[todo_ref[j]] = inner_ref[j]

    def convolve(i):
        tile, first = todo_ref[known + i // chunks], i % chunks * chunk
        values = transposed_convolution(tile, first, chunk, grid_ref, w_ref, pads_ref)
        all_ref[tile, pl.ds(first, chunk)] = values

    repeat((tiles - known) * chunks, 4, convolve)
    local = tap_refs[0].shape[1] // (sections * micros)
    band = BAND_ROWS * BAND_COLS
    for k, tap_ref in enumerate(tap_refs):
        source = lax.rem(group_ref[0] - k + groups, groups)
        for part in range(sections):
            tile, inside = divmod(part * local, band)
            row, col = divmod(inside, BAND_COLS)
            for micro in range(micros):
                at = (part * micros + micro) * local
                right_ref[at : at + local, :] = all_ref[
                    micro * TILE_CAP + tile, source * BAND_ROWS + row, col : col + local, :
                ]
        product = jnp.dot(tap_ref[...], right_ref[...], preferred_element_type=jnp.float32)
        lateral_ref[...] = product if k == 0 else lateral_ref[...] + product


def write_shifts(value, rows, cols, pads_ref):
    count = rows * cols
    col = lax.broadcasted_iota(jnp.int32, value.shape, 0) % cols
    zeros = jnp.zeros((cols, value.shape[1]), jnp.float32)
    left = jnp.where(col == 0, 0.0, pltpu.roll(value, 1, 0))
    right = jnp.where(col == cols - 1, 0.0, pltpu.roll(value, count - 1, 0))
    for j, moved in enumerate((left, value, right)):
        pads_ref[j, 0:cols, :] = zeros
        pads_ref[j, cols : cols + count, :] = moved
        pads_ref[j, cols + count : count + 2 * cols, :] = zeros


def write_owned(pads_ref, j, rows, cols, own_start, out_ref):
    own_cols = out_ref.shape[0] // rows
    for row in range(rows):
        at = pl.multiple_of(cols + row * cols + own_start, 8)
        out_ref[row * own_cols : (row + 1) * own_cols, :] = pads_ref[j, pl.ds(at, own_cols), :].astype(jnp.bfloat16)


def forward_kernel(
    section, rows, cols, place_ref, x_ref, lateral_ref, w_ref, old_ref, out_ref, preact_ref, summed_ref, pads_ref
):
    chans = w_ref.shape[1]
    count = rows * cols

    @pl.when(place_ref[0] == section)
    def _():
        summed = lateral_ref[:, :chans].astype(jnp.float32)
        if section:
            summed = x_ref[...].astype(jnp.float32) + summed
        summed = summed.astype(jnp.bfloat16).astype(jnp.float32)
        write_shifts(summed, rows, cols, pads_ref)
        write_owned(pads_ref, 1, rows, cols, place_ref[1], summed_ref)
        total = jnp.zeros((count, chans), jnp.float32)
        for offset, (dr, dc) in enumerate(neighbour_shifts()):
            lhs = pads_ref[dc + 1, (1 + dr) * cols : (1 + dr) * cols + count, :].astype(jnp.bfloat16)
            total = total + jnp.dot(lhs, w_ref[offset * chans : (offset + 1) * chans, :], preferred_element_type=jnp.float32)
        preact_ref[...] = total
        out_ref[...] = (total / (1.0 + jnp.exp(-total))).astype(jnp.bfloat16)

    @pl.when(place_ref[0] != section)
    def _():
        summed_ref[...] = old_ref[...]


def backward_kernel(section, rows, cols, classes, weight_unit, has_loss, place_ref, in_ref, preact_ref, w_ref, old_ref, *refs):
    if has_loss:
        classifier_ref, marks_ref, *refs = refs
    *out_refs, pre_ref, pads_ref = refs
    chans = preact_ref.shape[1]
    count = rows * cols

    @pl.when(place_ref[0] == section)
    def _():
        preact = preact_ref[...]
        if has_loss:
            logits = jnp.dot(in_ref[...], classifier_ref[...], preferred_element_type=jnp.float32)
            ids = lax.broadcasted_iota(jnp.int32, logits.shape, 1)
            expo = jnp.where(ids < classes, jnp.exp(logits), 0.0)
            probs = expo / jnp.sum(expo, axis=-1, keepdims=True)
            marks = marks_ref[:, chans : chans + MARKS].astype(jnp.float32)
            onehot = (marks[:, 0:1].astype(jnp.int32) == ids).astype(jnp.float32)
            weight = marks[:, 2:3] / marks[:, 1:2] * weight_unit
            grad_logits = ((probs - onehot) * weight).astype(jnp.bfloat16)
            grad_out = lax.dot_general(
                grad_logits, classifier_ref[...], (((1,), (1,)), ((), ())), preferred_element_type=jnp.float32
            )
        else:
            grad_out = in_ref[...].astype(jnp.float32)
        sigma = 1.0 / (1.0 + jnp.exp(-preact))
        grad_pre = (grad_out * sigma * (1.0 + preact * (1.0 - sigma))).astype(jnp.bfloat16)
        write_shifts(grad_pre.astype(jnp.float32), rows, cols, pads_ref)
        write_owned(pads_ref, 1, rows, cols, place_ref[1], pre_ref)
        if section:
            total = jnp.zeros((count, chans), jnp.float32)
            for offset, (dr, dc) in enumerate(neighbour_shifts()):
                lhs = pads_ref[1 - dc, (1 - dr) * cols : (1 - dr) * cols + count, :].astype(jnp.bfloat16)
                total = total + lax.dot_general(
                    lhs,
                    w_ref[offset * chans : (offset + 1) * chans, :],
                    (((1,), (1,)), ((), ())),
                    preferred_element_type=jnp.float32,
                )
            out_refs[0][...] = total.astype(jnp.bfloat16)

    @pl.when(place_ref[0] != section)
    def _():
        pre_ref[...] = old_ref[...]


def on_device(tap_maps, lateral_weight, conv_weight, classifier, tile_counts, labels):
    sections = lax.axis_size("section")
    groups = lax.axis_size("dp")
    place = lax.axis_index("section")
    group = lax.axis_index("dp")
    levels, micros, local, width = tap_maps.shape
    pixels = labels.shape[1]
    chans = conv_weight.shape[2]
    classes = classifier.shape[1]
    tiles = micros * TILE_CAP
    rows = groups * BAND_ROWS
    strips = groups // tiles
    own_cols = BAND_COLS // strips
    reach = -(-2 * sections // 8) * 8
    if strips == 1:
        cols = own_cols
    elif strips == 2:
        cols = own_cols + reach
    else:
        cols = min(BAND_COLS, own_cols + 2 * reach)
    starts = [min(max(h * own_cols - reach, 0), BAND_COLS - cols) for h in range(strips)]
    order = ring_order(groups)
    places = [order.index(device) for device in range(groups)]
    own_start = by_device([(p % strips) * own_cols - starts[p % strips] for p in range(groups)])
    count = rows * cols
    vmem = pl.BlockSpec(memory_space=pltpu.VMEM)
    smem = pl.BlockSpec(memory_space=pltpu.SMEM)
    weights = conv_weight[0]

    def windows(field):
        grid = field.reshape(tiles, BAND_ROWS, BAND_COLS, field.shape[-1])
        parts = [grid[p // strips, :, starts[p % strips] : starts[p % strips] + cols] for p in places]
        return jnp.stack(parts)

    chosen = tap_maps if sections == levels else tap_maps[jnp.array([s * levels // sections for s in range(sections)])]
    depth = width // groups
    taps = lax.all_to_all(chosen, "section", 0, 0, tiled=True).reshape(sections * micros * local, width)
    taps = taps.T.reshape(groups, depth, sections * micros * local)
    ring = Ring(lateral_weight[0])
    while ring.done < ring.steps - 2:
        ring.step()
    taps = ring.after(taps)
    ring.finish()
    lateral = pl.pallas_call(
        lateral_kernel,
        out_shape=jax.ShapeDtypeStruct((sections * micros * local, chans), jnp.bfloat16),
        in_specs=[smem] + [vmem] * (1 + len(ring.blocks)),
        out_specs=vmem,
        scratch_shapes=[pltpu.VMEM((sections * micros * local, chans), jnp.float32)],
        compiler_params=pltpu.CompilerParams(vmem_limit_bytes=16 << 20),
    )(jnp.array(order, jnp.int32)[ring.sources], taps, *ring.blocks)
    lateral = lateral.reshape(sections, micros, local, chans).transpose(1, 0, 2, 3)
    lateral = lateral.reshape(micros, pixels, chans)
    band = BAND_ROWS * BAND_COLS
    counts = jnp.broadcast_to(tile_counts[0][:, None], (micros, pixels))
    valid = (jnp.arange(pixels) // band)[None, :] < counts
    marks = jnp.stack([labels, counts, valid.astype(jnp.int32)], axis=-1).astype(jnp.bfloat16)
    marks = jnp.pad(marks, ((0, 0), (0, 0), (0, MARKS - 3)))
    lateral = windows(jnp.concatenate([lateral, marks], axis=-1))
    lateral = lax.all_to_all(lateral, "dp", 0, 0, tiled=True).reshape(count, chans + MARKS)
    weight_unit = 1.0 / (band * groups * micros)
    padded_classes = -(-classes // 128) * 128
    wide_classifier = jnp.pad(classifier, ((0, 0), (0, padded_classes - classes)))

    params = pltpu.CompilerParams(vmem_limit_bytes=(10 << 20) + 50 * count * chans)
    pads = pltpu.VMEM((3, count + 2 * cols, chans), jnp.float32)
    half = jax.ShapeDtypeStruct((count, chans), jnp.bfloat16)
    full = jax.ShapeDtypeStruct((count, chans), jnp.float32)
    own = jax.ShapeDtypeStruct((rows * own_cols, chans), jnp.bfloat16)
    where = jnp.stack([place, own_start]).astype(jnp.int32)
    summed = jnp.zeros(own.shape, own.dtype)
    grads = jnp.zeros(own.shape, own.dtype)

    turned = lax.dynamic_slice_in_dim(jnp.concatenate([taps, taps]), group, groups, axis=0)
    taps_to = [turned[k] for k in range(groups)]

    lateral, where, wide_classifier, summed, grads, taps_to = lax.optimization_barrier(
        (lateral, where, wide_classifier, summed, grads, taps_to)
    )
    taps_from = [taps_to[0]]
    for k in range(1, groups):
        taps_from.append(lax.ppermute(taps_to[k], "dp", [(i, (i + k) % groups) for i in range(groups)]))

    carried = lateral
    preact_of = []
    for section in range(sections):
        if section:
            ready = (groups - 1) * (section - 1) // (sections - 1) + 1
            carried, taps_from[:ready] = lax.optimization_barrier((carried, taps_from[:ready]))
            carried = lax.ppermute(carried, "section", [(section - 1, section)])
        carried, preact, summed = pl.pallas_call(
            functools.partial(forward_kernel, section, rows, cols),
            out_shape=(half, full, own),
            in_specs=[smem] + [vmem] * 4,
            out_specs=(vmem,) * 3,
            scratch_shapes=[pads],
            compiler_params=params,
        )(where, carried, lateral, weights, summed)
        preact_of.append(preact)

    summed_ring = Ring(summed.reshape(rows, own_cols, chans))
    for section in range(sections - 1, -1, -1):
        has_loss = section == sections - 1
        extra = (wide_classifier, lateral) if has_loss else ()
        carried, taps_from = lax.optimization_barrier((summed_ring.after(carried), taps_from))
        summed_ring.step()
        if not has_loss:
            carried = lax.ppermute(carried, "section", [(section + 1, section)])
        *carried, grads = pl.pallas_call(
            functools.partial(backward_kernel, section, rows, cols, classes, weight_unit, has_loss),
            out_shape=(half, own) if section else (own,),
            in_specs=[smem] + [vmem] * (4 + len(extra)),
            out_specs=(vmem,) * (2 if section else 1),
            scratch_shapes=[pads],
            compiler_params=params,
        )(where, carried, preact_of[section], weights, grads, *extra)
        carried = carried[0] if section else None
    summed_ring.finish()
    grads, summed_ring.blocks, taps_from = lax.optimization_barrier((grads, summed_ring.blocks, taps_from))

    ring = Ring(grads.reshape(rows, own_cols, chans))
    ring.step()

    chunk = min(rows, 8)
    grid_shape = pltpu.VMEM((tiles, rows + 2, strips, own_cols, chans), jnp.bfloat16)
    share = 9 * chans // groups
    pieces = max(-(-(g * share % chans + share) // chans) for g in range(groups))
    spot = jnp.stack([group * share // chans, group * share % chans]).astype(jnp.int32)
    params = pltpu.CompilerParams(vmem_limit_bytes=(16 << 20) + 8 * groups * rows * own_cols * chans)
    columns = pl.pallas_call(
        functools.partial(columns_kernel, rows, strips, chunk),
        out_shape=jax.ShapeDtypeStruct((tiles, rows // chunk, share, chunk * BAND_COLS), jnp.bfloat16),
        in_specs=[smem] * 2 + [vmem] * len(summed_ring.blocks),
        out_specs=vmem,
        scratch_shapes=[
            grid_shape,
            pltpu.VMEM((3, (chunk + 2) * BAND_COLS, chans), jnp.float32),
            pltpu.VMEM((pieces * chans, chunk * BAND_COLS), jnp.float32),
        ],
        compiler_params=params,
    )(summed_ring.sources, spot, *summed_ring.blocks)

    todo = []
    for p in range(groups):
        last = sorted({((p + far) % groups) // strips for far in (groups // 2 - 1, groups // 2 + 1)})
        rest = [t for t in range(tiles) if t not in last]
        todo.append((rest + last) if len(last) == 2 else (rest[1:] + rest[:1] + last))
    todo = by_device(todo)
    while ring.done < ring.steps - 2:
        ring.step()
    arrived = list(ring.blocks)
    columns = ring.after(columns)
    ring.step()
    chunk_shape = pltpu.VMEM((3, (chunk + 2) * BAND_COLS, chans), jnp.bfloat16)
    inner = pl.pallas_call(
        functools.partial(early_gradient_kernel, rows, strips, chunk),
        out_shape=jax.ShapeDtypeStruct((tiles - 2, rows, BAND_COLS, chans), jnp.bfloat16),
        in_specs=[smem] * 2 + [vmem] * (1 + len(arrived)),
        out_specs=vmem,
        scratch_shapes=[grid_shape, chunk_shape],
        compiler_params=params,
    )(ring.sources, todo, weights, *arrived)
    inner = ring.after(inner)
    ring.finish()
    conv_grad, lateral_grad = pl.pallas_call(
        functools.partial(late_gradient_kernel, rows, strips, chunk, sections, micros),
        out_shape=(
            jax.ShapeDtypeStruct((share, chans), jnp.float32),
            jax.ShapeDtypeStruct((depth, chans), jnp.float32),
        ),
        in_specs=[smem] * 3 + [vmem] * (3 + len(taps_from) + len(ring.blocks)),
        out_specs=(vmem, vmem),
        scratch_shapes=[
            grid_shape,
            chunk_shape,
            pltpu.VMEM((tiles, rows, BAND_COLS, chans), jnp.bfloat16),
            pltpu.VMEM((sections * micros * local, chans), jnp.bfloat16),
        ],
        compiler_params=params,
    )(ring.sources, todo, group.reshape(1), weights, columns, inner, *taps_from, *ring.blocks)
    return (conv_grad[None], lateral_grad[None])


def solution(mesh):
    placed = (
        P(None, None, ("dp", "section"), None),
        P("section", "dp", None),
        P("section", None, None),
        P(),
        P("dp", None),
        P(None, "dp"),
    )
    return jax.shard_map(
        on_device,
        mesh=mesh,
        in_specs=placed,
        out_specs=(P("section", "dp", None), P("section", "dp", None)),
        check_vma=False,
    )
```

```python
import functools

import jax
import jax.numpy as jnp
from jax import lax
from jax.experimental import pallas as pl
from jax.experimental.pallas import tpu as pltpu
from jax.sharding import PartitionSpec as P

TILE_CAP = 2
BAND_ROWS = 1
BAND_COLS = 64
MARKS = 128


def neighbour_shifts():
    return [(row_shift, col_shift) for row_shift in (-1, 0, 1) for col_shift in (-1, 0, 1)]


def ring_order(groups):
    return list(range(0, groups, 2)) + list(range(1, groups, 2))[::-1]


def by_device(per_place):
    groups = len(per_place)
    order = ring_order(groups)
    listed = [per_place[order.index(device)] for device in range(groups)]
    return lax.dynamic_index_in_dim(jnp.array(listed, jnp.int32), lax.axis_index("dp"), 0, keepdims=False)


class Ring:
    def __init__(self, block):
        groups = lax.axis_size("dp")
        order = ring_order(groups)
        self.steps = groups // 2
        self.up_route = [(order[i], order[(i + 1) % groups]) for i in range(groups)]
        self.down_route = [(j, i) for i, j in self.up_route]
        self.done = 0
        self.up = self.down = block
        self.blocks = [block]
        steps = [sign * step for step in range(1, self.steps) for sign in (-1, 1)]
        self.sources = by_device([[(spot + shift) % groups for shift in [0] + steps + [self.steps]] for spot in range(groups)])

    def after(self, other):
        self.up, self.down, other = lax.optimization_barrier((self.up, self.down, other))
        return other

    def step(self):
        self.done += 1
        if self.done < self.steps:
            self.up = lax.ppermute(self.up, "dp", self.up_route)
            self.down = lax.ppermute(self.down, "dp", self.down_route)
        elif self.done == self.steps:
            sections = lax.axis_size("section")
            axes = ("dp", "section")
            for_even = [(i * sections + s, j * sections + s) for i, j in self.up_route for s in range(0, sections, 2)]
            for_odd = [(i * sections + s, j * sections + s) for i, j in self.down_route for s in range(1, sections, 2)]
            self.up = lax.ppermute(self.up, axes, for_even)
            self.down = lax.ppermute(self.down, axes, for_odd)
        else:
            return
        self.blocks += [self.up, self.down]

    def finish(self):
        while self.done < self.steps:
            self.step()


def lateral_kernel(pieces, sources_ref, taps_ref, marks_ref, *refs):
    *block_refs, out_ref, total_ref = refs
    groups = taps_ref.shape[0]
    chans = total_ref.shape[1]
    contract = (((0,), (0,)), ((), ()))
    for k in range(groups):
        block = block_refs[k][...] if k < groups - 1 else block_refs[k][...] + block_refs[k + 1][...]
        product = lax.dot_general(taps_ref[sources_ref[k]], block, contract, preferred_element_type=jnp.float32)
        total_ref[...] = product if k == 0 else total_ref[...] + product
    for j, runs in enumerate(pieces):
        window = jnp.concatenate([total_ref[at : at + size, :] for at, size in runs])
        out_ref[j, :, :chans] = window.astype(jnp.bfloat16)
        out_ref[j, :, chans:] = marks_ref[j]


def repeat(times, unrolled, body):
    if times <= unrolled:
        for i in range(times):
            body(i)
    else:
        lax.fori_loop(0, times, lambda i, _: body(i), None)


def assemble(rows, strips, sources_ref, block_refs, grid_ref):
    blank = jnp.zeros((grid_ref.shape[0],) + grid_ref.shape[2:], grid_ref.dtype)
    grid_ref[:, 0] = blank
    grid_ref[:, rows + 1] = blank
    groups = sources_ref.shape[0]
    for k, block_ref in enumerate(block_refs[:groups]):
        source = sources_ref[k]

        def copy_row(row, k=k, block_ref=block_ref, source=source):
            block = block_ref[row] + block_refs[groups][row] if k == groups - 1 else block_ref[row]
            grid_ref[source // strips, 1 + row, source % strips] = block

        repeat(rows, 8, copy_row)


def transposed_convolution(tile, first, chunk, grid_ref, w_ref, pads_ref):
    chans = grid_ref.shape[4]
    size = (chunk + 2) * BAND_COLS
    value = grid_ref[tile, pl.ds(first, chunk + 2)].reshape(size, chans).astype(jnp.float32)
    col = lax.broadcasted_iota(jnp.int32, value.shape, 0) % BAND_COLS
    pads_ref[0] = jnp.where(col == 0, 0.0, pltpu.roll(value, 1, 0)).astype(jnp.bfloat16)
    pads_ref[1] = value.astype(jnp.bfloat16)
    pads_ref[2] = jnp.where(col == BAND_COLS - 1, 0.0, pltpu.roll(value, size - 1, 0)).astype(jnp.bfloat16)
    total = jnp.zeros((chunk * BAND_COLS, chans), jnp.float32)
    for offset, (dr, dc) in enumerate(neighbour_shifts()):
        total = total + lax.dot_general(
            pads_ref[1 - dc, (1 - dr) * BAND_COLS : (1 - dr + chunk) * BAND_COLS, :],
            w_ref[offset * chans : (offset + 1) * chans, :],
            (((1,), (1,)), ((), ())),
            preferred_element_type=jnp.float32,
        )
    return total.astype(jnp.bfloat16).reshape(chunk, BAND_COLS, chans)


def columns_kernel(rows, strips, chunk, sources_ref, spot_ref, *refs):
    *block_refs, out_ref, grid_ref, pads_ref, wide_ref = refs
    tiles, _, share = out_ref.shape[:3]
    chans = grid_ref.shape[4]
    assemble(rows, strips, sources_ref, block_refs, grid_ref)
    size = (chunk + 2) * BAND_COLS
    chunks = rows // chunk

    def fill(i):
        tile, first = i // chunks, i % chunks * chunk
        value = grid_ref[tile, pl.ds(first, chunk + 2)].reshape(size, chans).astype(jnp.float32)
        col = lax.broadcasted_iota(jnp.int32, value.shape, 0) % BAND_COLS
        pads_ref[0] = jnp.where(col == 0, 0.0, pltpu.roll(value, 1, 0))
        pads_ref[1] = value
        pads_ref[2] = jnp.where(col == BAND_COLS - 1, 0.0, pltpu.roll(value, size - 1, 0))
        for piece in range(wide_ref.shape[0] // chans):
            offset = jnp.minimum(spot_ref[0] + piece, 8)
            at = pl.multiple_of(offset // 3 * BAND_COLS, BAND_COLS)
            moved = pads_ref[offset % 3, pl.ds(at, chunk * BAND_COLS), :]
            wide_ref[piece * chans : (piece + 1) * chans, :] = moved.T
        part = wide_ref[pl.ds(pl.multiple_of(spot_ref[1], 8), share), :]
        out_ref[tile, i % chunks] = part.astype(jnp.bfloat16)

    repeat(tiles * chunks, 4, fill)


def early_gradient_kernel(rows, strips, chunk, which, sources_ref, todo_ref, w_ref, *refs):
    *block_refs, inner_ref, grid_ref, pads_ref = refs
    assemble(rows, strips, sources_ref, block_refs, grid_ref)

    def convolve(i):
        first = i * chunk
        inner_ref[pl.ds(first, chunk)] = transposed_convolution(todo_ref[which], first, chunk, grid_ref, w_ref, pads_ref)

    repeat(rows // chunk, 4, convolve)


def late_gradient_kernel(
    rows, strips, chunk, sections, micros, sources_ref, todo_ref, group_ref, w_ref, columns_ref, *refs
):
    *other_refs, conv_ref, lateral_ref, grid_ref, pads_ref, all_ref, right_ref = refs
    tiles, groups = grid_ref.shape[0], sources_ref.shape[0]
    known = tiles - 2
    inner_refs, tap_refs, block_refs = other_refs[:known], other_refs[known : known + groups], other_refs[known + groups :]
    chans = grid_ref.shape[4]
    assemble(rows, strips, sources_ref, block_refs, grid_ref)
    chunks = rows // chunk
    conv_ref[...] = jnp.zeros_like(conv_ref)

    def multiply(i):
        right = grid_ref[i // chunks, pl.ds(1 + i % chunks * chunk, chunk)].reshape(chunk * BAND_COLS, chans)
        conv_ref[...] += jnp.dot(columns_ref[i // chunks, i % chunks], right, preferred_element_type=jnp.float32)

    repeat(tiles * chunks, 4, multiply)
    for j, inner_ref in enumerate(inner_refs):
        all_ref[todo_ref[j]] = inner_ref[...]

    def convolve(i):
        tile, first = todo_ref[known + i // chunks], i % chunks * chunk
        values = transposed_convolution(tile, first, chunk, grid_ref, w_ref, pads_ref)
        all_ref[tile, pl.ds(first, chunk)] = values

    repeat((tiles - known) * chunks, 4, convolve)
    local = tap_refs[0].shape[1] // (sections * micros)
    band = BAND_ROWS * BAND_COLS
    for k, tap_ref in enumerate(tap_refs):
        source = lax.rem(group_ref[0] - k + groups, groups)
        for part in range(sections):
            tile, inside = divmod(part * local, band)
            row, col = divmod(inside, BAND_COLS)
            for micro in range(micros):
                at = (part * micros + micro) * local
                right_ref[at : at + local, :] = all_ref[
                    micro * TILE_CAP + tile, source * BAND_ROWS + row, col : col + local, :
                ]
        product = jnp.dot(tap_ref[...], right_ref[...], preferred_element_type=jnp.float32)
        lateral_ref[...] = product if k == 0 else lateral_ref[...] + product


def write_shifts(value, rows, cols, pads_ref):
    count = rows * cols
    col = lax.broadcasted_iota(jnp.int32, value.shape, 0) % cols
    zeros = jnp.zeros((cols, value.shape[1]), jnp.float32)
    left = jnp.where(col == 0, 0.0, pltpu.roll(value, 1, 0))
    right = jnp.where(col == cols - 1, 0.0, pltpu.roll(value, count - 1, 0))
    for j, moved in enumerate((left, value, right)):
        pads_ref[j, 0:cols, :] = zeros
        pads_ref[j, cols : cols + count, :] = moved
        pads_ref[j, cols + count : count + 2 * cols, :] = zeros


def write_owned(pads_ref, j, rows, cols, own_start, out_ref):
    own_cols = out_ref.shape[0] // rows
    for row in range(rows):
        at = pl.multiple_of(cols + row * cols + own_start, 8)
        out_ref[row * own_cols : (row + 1) * own_cols, :] = pads_ref[j, pl.ds(at, own_cols), :].astype(jnp.bfloat16)


def forward_kernel(
    section, rows, cols, place_ref, x_ref, lateral_ref, w_ref, old_ref, out_ref, preact_ref, summed_ref, pads_ref
):
    chans = w_ref.shape[1]
    count = rows * cols

    @pl.when(place_ref[0] == section)
    def _():
        summed = lateral_ref[:, :chans].astype(jnp.float32)
        if section:
            summed = x_ref[...].astype(jnp.float32) + summed
        summed = summed.astype(jnp.bfloat16).astype(jnp.float32)
        write_shifts(summed, rows, cols, pads_ref)
        write_owned(pads_ref, 1, rows, cols, place_ref[1], summed_ref)
        total = jnp.zeros((count, chans), jnp.float32)
        for offset, (dr, dc) in enumerate(neighbour_shifts()):
            lhs = pads_ref[dc + 1, (1 + dr) * cols : (1 + dr) * cols + count, :].astype(jnp.bfloat16)
            total = total + jnp.dot(lhs, w_ref[offset * chans : (offset + 1) * chans, :], preferred_element_type=jnp.float32)
        preact_ref[...] = total
        out_ref[...] = (total / (1.0 + jnp.exp(-total))).astype(jnp.bfloat16)

    @pl.when(place_ref[0] != section)
    def _():
        summed_ref[...] = old_ref[...]


def backward_kernel(section, rows, cols, classes, weight_unit, has_loss, place_ref, in_ref, preact_ref, w_ref, old_ref, *refs):
    if has_loss:
        classifier_ref, marks_ref, *refs = refs
    *out_refs, pre_ref, pads_ref = refs
    chans = preact_ref.shape[1]
    count = rows * cols

    @pl.when(place_ref[0] == section)
    def _():
        preact = preact_ref[...]
        if has_loss:
            logits = jnp.dot(in_ref[...], classifier_ref[...], preferred_element_type=jnp.float32)
            ids = lax.broadcasted_iota(jnp.int32, logits.shape, 1)
            expo = jnp.where(ids < classes, jnp.exp(logits), 0.0)
            probs = expo / jnp.sum(expo, axis=-1, keepdims=True)
            marks = marks_ref[:, chans : chans + MARKS].astype(jnp.float32)
            onehot = (marks[:, 0:1].astype(jnp.int32) == ids).astype(jnp.float32)
            weight = marks[:, 2:3] / marks[:, 1:2] * weight_unit
            grad_logits = ((probs - onehot) * weight).astype(jnp.bfloat16)
            grad_out = lax.dot_general(
                grad_logits, classifier_ref[...], (((1,), (1,)), ((), ())), preferred_element_type=jnp.float32
            )
        else:
            grad_out = in_ref[...].astype(jnp.float32)
        sigma = 1.0 / (1.0 + jnp.exp(-preact))
        grad_pre = (grad_out * sigma * (1.0 + preact * (1.0 - sigma))).astype(jnp.bfloat16)
        write_shifts(grad_pre.astype(jnp.float32), rows, cols, pads_ref)
        write_owned(pads_ref, 1, rows, cols, place_ref[1], pre_ref)
        if section:
            total = jnp.zeros((count, chans), jnp.float32)
            for offset, (dr, dc) in enumerate(neighbour_shifts()):
                lhs = pads_ref[1 - dc, (1 - dr) * cols : (1 - dr) * cols + count, :].astype(jnp.bfloat16)
                total = total + lax.dot_general(
                    lhs,
                    w_ref[offset * chans : (offset + 1) * chans, :],
                    (((1,), (1,)), ((), ())),
                    preferred_element_type=jnp.float32,
                )
            out_refs[0][...] = total.astype(jnp.bfloat16)

    @pl.when(place_ref[0] != section)
    def _():
        pre_ref[...] = old_ref[...]


def on_device(tap_maps, lateral_weight, conv_weight, classifier, tile_counts, labels):
    sections = lax.axis_size("section")
    groups = lax.axis_size("dp")
    place = lax.axis_index("section")
    group = lax.axis_index("dp")
    levels, micros, local, width = tap_maps.shape
    pixels = labels.shape[1]
    chans = conv_weight.shape[2]
    classes = classifier.shape[1]
    tiles = micros * TILE_CAP
    rows = groups * BAND_ROWS
    strips = groups // tiles
    own_cols = BAND_COLS // strips
    reach = -(-2 * sections // 8) * 8
    if strips == 1:
        cols = own_cols
    elif strips == 2:
        cols = own_cols + reach
    else:
        cols = min(BAND_COLS, own_cols + 2 * reach)
    starts = [min(max(h * own_cols - reach, 0), BAND_COLS - cols) for h in range(strips)]
    order = ring_order(groups)
    places = [order.index(device) for device in range(groups)]
    own_start = by_device([(p % strips) * own_cols - starts[p % strips] for p in range(groups)])
    count = rows * cols
    vmem = pl.BlockSpec(memory_space=pltpu.VMEM)
    smem = pl.BlockSpec(memory_space=pltpu.SMEM)
    weights = conv_weight[0]

    def windows(field):
        grid = field.reshape(tiles, BAND_ROWS, BAND_COLS, field.shape[-1])
        parts = [grid[p // strips, :, starts[p % strips] : starts[p % strips] + cols] for p in places]
        return jnp.stack(parts)

    chosen = tap_maps if sections == levels else tap_maps[jnp.array([s * levels // sections for s in range(sections)])]
    depth = width // groups
    taps = lax.all_to_all(chosen, "section", 0, 0, tiled=True).reshape(sections * micros * local, width)
    taps = taps.T.reshape(groups, depth, sections * micros * local)
    ring = Ring(lateral_weight[0])
    while ring.done < ring.steps - 2:
        ring.step()
    band = BAND_ROWS * BAND_COLS
    counts = jnp.broadcast_to(tile_counts[0][:, None], (micros, pixels))
    valid = (jnp.arange(pixels) // band)[None, :] < counts
    marks = jnp.stack([labels, counts, valid.astype(jnp.int32)], axis=-1).astype(jnp.bfloat16)
    marks = windows(jnp.pad(marks, ((0, 0), (0, 0), (0, MARKS - 3)))).reshape(groups, BAND_ROWS * cols, MARKS)
    runs = []
    for p in places:
        micro, tile = divmod(p // strips, TILE_CAP)
        runs.append([])
        for row in range(BAND_ROWS):
            at = tile * band + row * BAND_COLS + starts[p % strips]
            end = at + cols
            while at < end:
                size = min(end - at, local - at % local)
                runs[-1].append(((at // local * micros + micro) * local + at % local, size))
                at += size
    last_tiles = [[((p + far) % groups) // strips for far in (groups // 2 - 1, groups // 2 + 1)] for p in range(groups)]
    todo = []
    for pair in last_tiles:
        last = sorted(set(pair))
        rest = [t for t in range(tiles) if t not in last]
        todo.append((rest + last) if len(last) == 2 else (rest[1:] + rest[:1] + last))
    todo = by_device(todo)
    share = 9 * chans // groups
    spot = jnp.stack([group * share // chans, group * share % chans]).astype(jnp.int32)
    mine = group.reshape(1)
    turned = lax.dynamic_slice_in_dim(jnp.concatenate([taps, taps]), group, groups, axis=0)
    taps_to = [turned[k] for k in range(groups)]

    taps, taps_to, marks, w_sources, todo, spot, mine = ring.after(
        (taps, taps_to, marks, jnp.array(order, jnp.int32)[ring.sources], todo, spot, mine)
    )
    ring.finish()
    lateral = pl.pallas_call(
        functools.partial(lateral_kernel, runs),
        out_shape=jax.ShapeDtypeStruct((groups, BAND_ROWS * cols, chans + MARKS), jnp.bfloat16),
        in_specs=[smem] + [vmem] * (2 + len(ring.blocks)),
        out_specs=vmem,
        scratch_shapes=[pltpu.VMEM((sections * micros * local, chans), jnp.float32)],
        compiler_params=pltpu.CompilerParams(vmem_limit_bytes=20 << 20),
    )(w_sources, taps, marks, *ring.blocks)
    lateral = lax.all_to_all(lateral, "dp", 0, 0, tiled=True).reshape(count, chans + MARKS)
    weight_unit = 1.0 / (band * groups * micros)
    padded_classes = -(-classes // 128) * 128
    wide_classifier = jnp.pad(classifier, ((0, 0), (0, padded_classes - classes)))

    params = pltpu.CompilerParams(vmem_limit_bytes=(10 << 20) + 50 * count * chans)
    pads = pltpu.VMEM((3, count + 2 * cols, chans), jnp.float32)
    half = jax.ShapeDtypeStruct((count, chans), jnp.bfloat16)
    full = jax.ShapeDtypeStruct((count, chans), jnp.float32)
    own = jax.ShapeDtypeStruct((rows * own_cols, chans), jnp.bfloat16)
    where = jnp.stack([place, own_start]).astype(jnp.int32)
    summed = jnp.zeros(own.shape, own.dtype)
    grads = jnp.zeros(own.shape, own.dtype)

    lateral, where, wide_classifier, summed, grads, taps_to, sources, todo, spot, mine = lax.optimization_barrier(
        (lateral, where, wide_classifier, summed, grads, taps_to, ring.sources, todo, spot, mine)
    )
    taps_from = [taps_to[0]]
    for k in range(1, groups):
        taps_from.append(lax.ppermute(taps_to[k], "dp", [(i, (i + k) % groups) for i in range(groups)]))

    carried = lateral
    preact_of = []
    for section in range(sections):
        if section:
            ready = (groups - 1) * (section - 1) // (sections - 1) + 1
            carried, taps_from[:ready] = lax.optimization_barrier((carried, taps_from[:ready]))
            carried = lax.ppermute(carried, "section", [(section - 1, section)])
        carried, preact, summed = pl.pallas_call(
            functools.partial(forward_kernel, section, rows, cols),
            out_shape=(half, full, own),
            in_specs=[smem] + [vmem] * 4,
            out_specs=(vmem,) * 3,
            scratch_shapes=[pads],
            compiler_params=params,
        )(where, carried, lateral, weights, summed)
        preact_of.append(preact)

    summed_ring = Ring(summed.reshape(rows, own_cols, chans))
    for section in range(sections - 1, -1, -1):
        has_loss = section == sections - 1
        extra = (wide_classifier, lateral) if has_loss else ()
        carried, taps_from = lax.optimization_barrier((summed_ring.after(carried), taps_from))
        summed_ring.step()
        if not has_loss:
            carried = lax.ppermute(carried, "section", [(section + 1, section)])
        *carried, grads = pl.pallas_call(
            functools.partial(backward_kernel, section, rows, cols, classes, weight_unit, has_loss),
            out_shape=(half, own) if section else (own,),
            in_specs=[smem] + [vmem] * (4 + len(extra)),
            out_specs=(vmem,) * (2 if section else 1),
            scratch_shapes=[pads],
            compiler_params=params,
        )(where, carried, preact_of[section], weights, grads, *extra)
        carried = carried[0] if section else None
    summed_ring.finish()
    grads, summed_ring.blocks, taps_from = lax.optimization_barrier((grads, summed_ring.blocks, taps_from))

    ring = Ring(grads.reshape(rows, own_cols, chans))
    ring.step()

    chunk = min(rows, 8)
    grid_shape = pltpu.VMEM((tiles, rows + 2, strips, own_cols, chans), jnp.bfloat16)
    pieces = max(-(-(g * share % chans + share) // chans) for g in range(groups))
    params = pltpu.CompilerParams(vmem_limit_bytes=(16 << 20) + 8 * groups * rows * own_cols * chans)
    columns = pl.pallas_call(
        functools.partial(columns_kernel, rows, strips, chunk),
        out_shape=jax.ShapeDtypeStruct((tiles, rows // chunk, share, chunk * BAND_COLS), jnp.bfloat16),
        in_specs=[smem] * 2 + [vmem] * len(summed_ring.blocks),
        out_specs=vmem,
        scratch_shapes=[
            grid_shape,
            pltpu.VMEM((3, (chunk + 2) * BAND_COLS, chans), jnp.float32),
            pltpu.VMEM((pieces * chans, chunk * BAND_COLS), jnp.float32),
        ],
        compiler_params=params,
    )(sources, spot, *summed_ring.blocks)

    while ring.done < ring.steps - 2:
        ring.step()
    arrived = list(ring.blocks)
    columns = ring.after(columns)
    ring.step()
    chunk_shape = pltpu.VMEM((3, (chunk + 2) * BAND_COLS, chans), jnp.bfloat16)

    def convolve_tile(which):
        return pl.pallas_call(
            functools.partial(early_gradient_kernel, rows, strips, chunk, which),
            out_shape=jax.ShapeDtypeStruct((rows, BAND_COLS, chans), jnp.bfloat16),
            in_specs=[smem] * 2 + [vmem] * (1 + len(arrived)),
            out_specs=vmem,
            scratch_shapes=[grid_shape, chunk_shape],
            compiler_params=params,
        )(sources, todo, weights, *arrived)

    inner = [convolve_tile(which) for which in range(tiles - 2)]
    inner[0] = ring.after(inner[0])
    ring.finish()
    conv_grad, lateral_grad = pl.pallas_call(
        functools.partial(late_gradient_kernel, rows, strips, chunk, sections, micros),
        out_shape=(
            jax.ShapeDtypeStruct((share, chans), jnp.float32),
            jax.ShapeDtypeStruct((depth, chans), jnp.float32),
        ),
        in_specs=[smem] * 3 + [vmem] * (2 + len(inner) + len(taps_from) + len(ring.blocks)),
        out_specs=(vmem, vmem),
        scratch_shapes=[
            grid_shape,
            chunk_shape,
            pltpu.VMEM((tiles, rows, BAND_COLS, chans), jnp.bfloat16),
            pltpu.VMEM((sections * micros * local, chans), jnp.bfloat16),
        ],
        compiler_params=params,
    )(sources, todo, mine, weights, columns, *inner, *taps_from, *ring.blocks)
    return (conv_grad[None], lateral_grad[None])


def solution(mesh):
    placed = (
        P(None, None, ("dp", "section"), None),
        P("section", "dp", None),
        P("section", None, None),
        P(),
        P("dp", None),
        P(None, "dp"),
    )
    return jax.shard_map(
        on_device,
        mesh=mesh,
        in_specs=placed,
        out_specs=(P("section", "dp", None), P("section", "dp", None)),
        check_vma=False,
    )
```

```python
import functools

import jax
import jax.numpy as jnp
from jax import lax
from jax.experimental import pallas as pl
from jax.experimental.pallas import tpu as pltpu
from jax.sharding import PartitionSpec as P

TILE_CAP = 2
BAND_ROWS = 1
BAND_COLS = 64
MARKS = 128


def neighbour_shifts():
    return [(row_shift, col_shift) for row_shift in (-1, 0, 1) for col_shift in (-1, 0, 1)]


def ring_order(groups):
    return list(range(0, groups, 2)) + list(range(1, groups, 2))[::-1]


def by_device(per_place):
    groups = len(per_place)
    order = ring_order(groups)
    listed = [per_place[order.index(device)] for device in range(groups)]
    return lax.dynamic_index_in_dim(jnp.array(listed, jnp.int32), lax.axis_index("dp"), 0, keepdims=False)


class Ring:
    def __init__(self, block):
        groups = lax.axis_size("dp")
        order = ring_order(groups)
        self.steps = groups // 2
        self.up_route = [(order[i], order[(i + 1) % groups]) for i in range(groups)]
        self.down_route = [(j, i) for i, j in self.up_route]
        self.done = 0
        self.up = self.down = block
        self.blocks = [block]
        steps = [sign * step for step in range(1, self.steps) for sign in (-1, 1)]
        self.sources = by_device([[(spot + shift) % groups for shift in [0] + steps + [self.steps]] for spot in range(groups)])

    def after(self, other):
        self.up, self.down, other = lax.optimization_barrier((self.up, self.down, other))
        return other

    def step(self):
        self.done += 1
        if self.done < self.steps:
            self.up = lax.ppermute(self.up, "dp", self.up_route)
            self.down = lax.ppermute(self.down, "dp", self.down_route)
        elif self.done == self.steps:
            sections = lax.axis_size("section")
            axes = ("dp", "section")
            for_even = [(i * sections + s, j * sections + s) for i, j in self.up_route for s in range(0, sections, 2)]
            for_odd = [(i * sections + s, j * sections + s) for i, j in self.down_route for s in range(1, sections, 2)]
            self.up = lax.ppermute(self.up, axes, for_even)
            self.down = lax.ppermute(self.down, axes, for_odd)
        else:
            return
        self.blocks += [self.up, self.down]

    def finish(self):
        while self.done < self.steps:
            self.step()


def lateral_kernel(pieces, sources_ref, taps_ref, marks_ref, *refs):
    *block_refs, out_ref, total_ref = refs
    groups = taps_ref.shape[0]
    chans = total_ref.shape[1]
    contract = (((0,), (0,)), ((), ()))
    for k in range(groups):
        block = block_refs[k][...] if k < groups - 1 else block_refs[k][...] + block_refs[k + 1][...]
        product = lax.dot_general(taps_ref[sources_ref[k]], block, contract, preferred_element_type=jnp.float32)
        total_ref[...] = product if k == 0 else total_ref[...] + product
    for j, runs in enumerate(pieces):
        window = jnp.concatenate([total_ref[at : at + size, :] for at, size in runs])
        out_ref[j, :, :chans] = window.astype(jnp.bfloat16)
        out_ref[j, :, chans:] = marks_ref[j]


def repeat(times, unrolled, body):
    if times <= unrolled:
        for i in range(times):
            body(i)
    else:
        lax.fori_loop(0, times, lambda i, _: body(i), None)


def assemble(rows, strips, sources_ref, block_refs, grid_ref):
    blank = jnp.zeros((grid_ref.shape[0],) + grid_ref.shape[2:], grid_ref.dtype)
    grid_ref[:, 0] = blank
    grid_ref[:, rows + 1] = blank
    groups = sources_ref.shape[0]
    for k, block_ref in enumerate(block_refs[:groups]):
        source = sources_ref[k]

        def copy_row(row, k=k, block_ref=block_ref, source=source):
            block = block_ref[row] + block_refs[groups][row] if k == groups - 1 else block_ref[row]
            grid_ref[source // strips, 1 + row, source % strips] = block

        repeat(rows, 8, copy_row)


def transposed_convolution(tile, first, chunk, grid_ref, w_ref, pads_ref):
    chans = grid_ref.shape[4]
    size = (chunk + 2) * BAND_COLS
    value = grid_ref[tile, pl.ds(first, chunk + 2)].reshape(size, chans).astype(jnp.float32)
    col = lax.broadcasted_iota(jnp.int32, value.shape, 0) % BAND_COLS
    pads_ref[0] = jnp.where(col == 0, 0.0, pltpu.roll(value, 1, 0)).astype(jnp.bfloat16)
    pads_ref[1] = value.astype(jnp.bfloat16)
    pads_ref[2] = jnp.where(col == BAND_COLS - 1, 0.0, pltpu.roll(value, size - 1, 0)).astype(jnp.bfloat16)
    total = jnp.zeros((chunk * BAND_COLS, chans), jnp.float32)
    for offset, (dr, dc) in enumerate(neighbour_shifts()):
        total = total + lax.dot_general(
            pads_ref[1 - dc, (1 - dr) * BAND_COLS : (1 - dr + chunk) * BAND_COLS, :],
            w_ref[offset * chans : (offset + 1) * chans, :],
            (((1,), (1,)), ((), ())),
            preferred_element_type=jnp.float32,
        )
    return total.astype(jnp.bfloat16).reshape(chunk, BAND_COLS, chans)


def columns_kernel(rows, strips, chunk, sources_ref, spot_ref, *refs):
    *block_refs, out_ref, grid_ref, pads_ref, wide_ref = refs
    tiles, _, share = out_ref.shape[:3]
    chans = grid_ref.shape[4]
    assemble(rows, strips, sources_ref, block_refs, grid_ref)
    size = (chunk + 2) * BAND_COLS
    chunks = rows // chunk

    def fill(i):
        tile, first = i // chunks, i % chunks * chunk
        value = grid_ref[tile, pl.ds(first, chunk + 2)].reshape(size, chans).astype(jnp.float32)
        col = lax.broadcasted_iota(jnp.int32, value.shape, 0) % BAND_COLS
        pads_ref[0] = jnp.where(col == 0, 0.0, pltpu.roll(value, 1, 0))
        pads_ref[1] = value
        pads_ref[2] = jnp.where(col == BAND_COLS - 1, 0.0, pltpu.roll(value, size - 1, 0))
        for piece in range(wide_ref.shape[0] // chans):
            offset = jnp.minimum(spot_ref[0] + piece, 8)
            at = pl.multiple_of(offset // 3 * BAND_COLS, BAND_COLS)
            moved = pads_ref[offset % 3, pl.ds(at, chunk * BAND_COLS), :]
            wide_ref[piece * chans : (piece + 1) * chans, :] = moved.T
        part = wide_ref[pl.ds(pl.multiple_of(spot_ref[1], 8), share), :]
        out_ref[tile, i % chunks] = part.astype(jnp.bfloat16)

    repeat(tiles * chunks, 4, fill)


def early_gradient_kernel(rows, strips, chunk, which, sources_ref, todo_ref, w_ref, *refs):
    *block_refs, inner_ref, grid_ref, pads_ref = refs
    assemble(rows, strips, sources_ref, block_refs, grid_ref)

    def convolve(i):
        first = i * chunk
        inner_ref[pl.ds(first, chunk)] = transposed_convolution(todo_ref[which], first, chunk, grid_ref, w_ref, pads_ref)

    repeat(rows // chunk, 4, convolve)


def late_gradient_kernel(
    rows, strips, chunk, sections, micros, sources_ref, todo_ref, group_ref, w_ref, columns_ref, *refs
):
    *other_refs, conv_ref, lateral_ref, grid_ref, pads_ref, all_ref, right_ref = refs
    tiles, groups = grid_ref.shape[0], sources_ref.shape[0]
    known = tiles - 2
    inner_refs, tap_refs, block_refs = other_refs[:known], other_refs[known : known + groups], other_refs[known + groups :]
    chans = grid_ref.shape[4]
    assemble(rows, strips, sources_ref, block_refs, grid_ref)
    chunks = rows // chunk

    def multiply(i):
        right = grid_ref[i // chunks, pl.ds(1 + i % chunks * chunk, chunk)].reshape(chunk * BAND_COLS, chans)
        product = jnp.dot(columns_ref[i // chunks, i % chunks], right, preferred_element_type=jnp.float32)
        conv_ref[...] = product if isinstance(i, int) and i == 0 else conv_ref[...] + product

    if tiles * chunks > 4:
        conv_ref[...] = jnp.zeros_like(conv_ref)
    repeat(tiles * chunks, 4, multiply)
    for j, inner_ref in enumerate(inner_refs):
        all_ref[todo_ref[j]] = inner_ref[...]

    def convolve(i):
        tile, first = todo_ref[known + i // chunks], i % chunks * chunk
        values = transposed_convolution(tile, first, chunk, grid_ref, w_ref, pads_ref)
        all_ref[tile, pl.ds(first, chunk)] = values

    repeat((tiles - known) * chunks, 4, convolve)
    local = tap_refs[0].shape[1] // (sections * micros)
    band = BAND_ROWS * BAND_COLS
    for k, tap_ref in enumerate(tap_refs):
        source = lax.rem(group_ref[0] - k + groups, groups)
        for part in range(sections):
            tile, inside = divmod(part * local, band)
            row, col = divmod(inside, BAND_COLS)
            for micro in range(micros):
                at = (part * micros + micro) * local
                right_ref[at : at + local, :] = all_ref[
                    micro * TILE_CAP + tile, source * BAND_ROWS + row, col : col + local, :
                ]
        product = jnp.dot(tap_ref[...], right_ref[...], preferred_element_type=jnp.float32)
        lateral_ref[...] = product if k == 0 else lateral_ref[...] + product


def write_shifts(value, rows, cols, pads_ref):
    count = rows * cols
    col = lax.broadcasted_iota(jnp.int32, value.shape, 0) % cols
    zeros = jnp.zeros((cols, value.shape[1]), jnp.float32)
    left = jnp.where(col == 0, 0.0, pltpu.roll(value, 1, 0))
    right = jnp.where(col == cols - 1, 0.0, pltpu.roll(value, count - 1, 0))
    for j, moved in enumerate((left, value, right)):
        pads_ref[j, 0:cols, :] = zeros
        pads_ref[j, cols : cols + count, :] = moved
        pads_ref[j, cols + count : count + 2 * cols, :] = zeros


def write_owned(pads_ref, j, rows, cols, own_start, out_ref):
    own_cols = out_ref.shape[0] // rows
    for row in range(rows):
        at = pl.multiple_of(cols + row * cols + own_start, 8)
        out_ref[row * own_cols : (row + 1) * own_cols, :] = pads_ref[j, pl.ds(at, own_cols), :].astype(jnp.bfloat16)


def forward_kernel(
    section, rows, cols, place_ref, x_ref, lateral_ref, w_ref, old_ref, out_ref, preact_ref, summed_ref, pads_ref
):
    chans = w_ref.shape[1]
    count = rows * cols

    @pl.when(place_ref[0] == section)
    def _():
        summed = lateral_ref[:, :chans].astype(jnp.float32)
        if section:
            summed = x_ref[...].astype(jnp.float32) + summed
        summed = summed.astype(jnp.bfloat16).astype(jnp.float32)
        write_shifts(summed, rows, cols, pads_ref)
        write_owned(pads_ref, 1, rows, cols, place_ref[1], summed_ref)
        total = jnp.zeros((count, chans), jnp.float32)
        for offset, (dr, dc) in enumerate(neighbour_shifts()):
            lhs = pads_ref[dc + 1, (1 + dr) * cols : (1 + dr) * cols + count, :].astype(jnp.bfloat16)
            total = total + jnp.dot(lhs, w_ref[offset * chans : (offset + 1) * chans, :], preferred_element_type=jnp.float32)
        preact_ref[...] = total
        out_ref[...] = (total / (1.0 + jnp.exp(-total))).astype(jnp.bfloat16)

    @pl.when(place_ref[0] != section)
    def _():
        summed_ref[...] = old_ref[...]


def backward_kernel(section, rows, cols, classes, weight_unit, has_loss, place_ref, in_ref, preact_ref, w_ref, old_ref, *refs):
    if has_loss:
        classifier_ref, marks_ref, *refs = refs
    *out_refs, pre_ref, pads_ref = refs
    chans = preact_ref.shape[1]
    count = rows * cols

    @pl.when(place_ref[0] == section)
    def _():
        preact = preact_ref[...]
        if has_loss:
            logits = jnp.dot(in_ref[...], classifier_ref[...], preferred_element_type=jnp.float32)
            ids = lax.broadcasted_iota(jnp.int32, logits.shape, 1)
            expo = jnp.where(ids < classes, jnp.exp(logits), 0.0)
            probs = expo / jnp.sum(expo, axis=-1, keepdims=True)
            marks = marks_ref[:, chans : chans + MARKS].astype(jnp.float32)
            onehot = (marks[:, 0:1].astype(jnp.int32) == ids).astype(jnp.float32)
            weight = marks[:, 2:3] / marks[:, 1:2] * weight_unit
            grad_logits = ((probs - onehot) * weight).astype(jnp.bfloat16)
            grad_out = lax.dot_general(
                grad_logits, classifier_ref[...], (((1,), (1,)), ((), ())), preferred_element_type=jnp.float32
            )
        else:
            grad_out = in_ref[...].astype(jnp.float32)
        sigma = 1.0 / (1.0 + jnp.exp(-preact))
        grad_pre = (grad_out * sigma * (1.0 + preact * (1.0 - sigma))).astype(jnp.bfloat16)
        write_shifts(grad_pre.astype(jnp.float32), rows, cols, pads_ref)
        write_owned(pads_ref, 1, rows, cols, place_ref[1], pre_ref)
        if section:
            total = jnp.zeros((count, chans), jnp.float32)
            for offset, (dr, dc) in enumerate(neighbour_shifts()):
                lhs = pads_ref[1 - dc, (1 - dr) * cols : (1 - dr) * cols + count, :].astype(jnp.bfloat16)
                total = total + lax.dot_general(
                    lhs,
                    w_ref[offset * chans : (offset + 1) * chans, :],
                    (((1,), (1,)), ((), ())),
                    preferred_element_type=jnp.float32,
                )
            out_refs[0][...] = total.astype(jnp.bfloat16)

    @pl.when(place_ref[0] != section)
    def _():
        pre_ref[...] = old_ref[...]


def on_device(tap_maps, lateral_weight, conv_weight, classifier, tile_counts, labels):
    sections = lax.axis_size("section")
    groups = lax.axis_size("dp")
    place = lax.axis_index("section")
    group = lax.axis_index("dp")
    levels, micros, local, width = tap_maps.shape
    pixels = labels.shape[1]
    chans = conv_weight.shape[2]
    classes = classifier.shape[1]
    tiles = micros * TILE_CAP
    rows = groups * BAND_ROWS
    strips = groups // tiles
    own_cols = BAND_COLS // strips
    reach = -(-2 * sections // 8) * 8
    if strips == 1:
        cols = own_cols
    elif strips == 2:
        cols = own_cols + reach
    else:
        cols = min(BAND_COLS, own_cols + 2 * reach)
    starts = [min(max(h * own_cols - reach, 0), BAND_COLS - cols) for h in range(strips)]
    order = ring_order(groups)
    places = [order.index(device) for device in range(groups)]
    own_start = by_device([(p % strips) * own_cols - starts[p % strips] for p in range(groups)])
    count = rows * cols
    vmem = pl.BlockSpec(memory_space=pltpu.VMEM)
    smem = pl.BlockSpec(memory_space=pltpu.SMEM)
    weights = conv_weight[0]

    def windows(field):
        grid = field.reshape(tiles, BAND_ROWS, BAND_COLS, field.shape[-1])
        parts = [grid[p // strips, :, starts[p % strips] : starts[p % strips] + cols] for p in places]
        return jnp.stack(parts)

    chosen = tap_maps if sections == levels else tap_maps[jnp.array([s * levels // sections for s in range(sections)])]
    depth = width // groups
    taps = lax.all_to_all(chosen, "section", 0, 0, tiled=True).reshape(sections * micros * local, width)
    taps = taps.T.reshape(groups, depth, sections * micros * local)
    ring = Ring(lateral_weight[0])
    while ring.done < ring.steps - 2:
        ring.step()
    band = BAND_ROWS * BAND_COLS
    counts = jnp.broadcast_to(tile_counts[0][:, None], (micros, pixels))
    valid = (jnp.arange(pixels) // band)[None, :] < counts
    marks = jnp.stack([labels, counts, valid.astype(jnp.int32)], axis=-1).astype(jnp.bfloat16)
    marks = windows(jnp.pad(marks, ((0, 0), (0, 0), (0, MARKS - 3)))).reshape(groups, BAND_ROWS * cols, MARKS)
    runs = []
    for p in places:
        micro, tile = divmod(p // strips, TILE_CAP)
        runs.append([])
        for row in range(BAND_ROWS):
            at = tile * band + row * BAND_COLS + starts[p % strips]
            end = at + cols
            while at < end:
                size = min(end - at, local - at % local)
                runs[-1].append(((at // local * micros + micro) * local + at % local, size))
                at += size
    last_tiles = [[((p + far) % groups) // strips for far in (groups // 2 - 1, groups // 2 + 1)] for p in range(groups)]
    todo = []
    for pair in last_tiles:
        last = sorted(set(pair))
        rest = [t for t in range(tiles) if t not in last]
        todo.append((rest + last) if len(last) == 2 else (rest[1:] + rest[:1] + last))
    todo = by_device(todo)
    share = 9 * chans // groups
    spot = jnp.stack([group * share // chans, group * share % chans]).astype(jnp.int32)
    mine = group.reshape(1)
    turned = lax.dynamic_slice_in_dim(jnp.concatenate([taps, taps]), group, groups, axis=0)
    taps_to = [turned[k] for k in range(groups)]

    taps, taps_to, marks, w_sources, todo, spot, mine = ring.after(
        (taps, taps_to, marks, jnp.array(order, jnp.int32)[ring.sources], todo, spot, mine)
    )
    ring.finish()
    lateral = pl.pallas_call(
        functools.partial(lateral_kernel, runs),
        out_shape=jax.ShapeDtypeStruct((groups, BAND_ROWS * cols, chans + MARKS), jnp.bfloat16),
        in_specs=[smem] + [vmem] * (2 + len(ring.blocks)),
        out_specs=vmem,
        scratch_shapes=[pltpu.VMEM((sections * micros * local, chans), jnp.float32)],
        compiler_params=pltpu.CompilerParams(vmem_limit_bytes=20 << 20),
    )(w_sources, taps, marks, *ring.blocks)
    lateral = lax.all_to_all(lateral, "dp", 0, 0, tiled=True).reshape(count, chans + MARKS)
    weight_unit = 1.0 / (band * groups * micros)
    padded_classes = -(-classes // 128) * 128
    wide_classifier = jnp.pad(classifier, ((0, 0), (0, padded_classes - classes)))

    params = pltpu.CompilerParams(vmem_limit_bytes=(10 << 20) + 50 * count * chans)
    pads = pltpu.VMEM((3, count + 2 * cols, chans), jnp.float32)
    half = jax.ShapeDtypeStruct((count, chans), jnp.bfloat16)
    full = jax.ShapeDtypeStruct((count, chans), jnp.float32)
    own = jax.ShapeDtypeStruct((rows * own_cols, chans), jnp.bfloat16)
    where = jnp.stack([place, own_start]).astype(jnp.int32)
    summed = jnp.zeros(own.shape, own.dtype)
    grads = jnp.zeros(own.shape, own.dtype)

    lateral, where, wide_classifier, summed, grads, taps_to, sources, todo, spot, mine = lax.optimization_barrier(
        (lateral, where, wide_classifier, summed, grads, taps_to, ring.sources, todo, spot, mine)
    )
    taps_from = [taps_to[0]]
    for k in range(1, groups):
        taps_from.append(lax.ppermute(taps_to[k], "dp", [(i, (i + k) % groups) for i in range(groups)]))

    carried = lateral
    preact_of = []
    for section in range(sections):
        if section:
            ready = (groups - 1) * (section - 1) // (sections - 1) + 1
            carried, taps_from[:ready] = lax.optimization_barrier((carried, taps_from[:ready]))
            carried = lax.ppermute(carried, "section", [(section - 1, section)])
        carried, preact, summed = pl.pallas_call(
            functools.partial(forward_kernel, section, rows, cols),
            out_shape=(half, full, own),
            in_specs=[smem] + [vmem] * 4,
            out_specs=(vmem,) * 3,
            scratch_shapes=[pads],
            compiler_params=params,
        )(where, carried, lateral, weights, summed)
        preact_of.append(preact)

    summed_ring = Ring(summed.reshape(rows, own_cols, chans))
    for section in range(sections - 1, -1, -1):
        has_loss = section == sections - 1
        extra = (wide_classifier, lateral) if has_loss else ()
        carried, taps_from = lax.optimization_barrier((summed_ring.after(carried), taps_from))
        summed_ring.step()
        if not has_loss:
            carried = lax.ppermute(carried, "section", [(section + 1, section)])
        *carried, grads = pl.pallas_call(
            functools.partial(backward_kernel, section, rows, cols, classes, weight_unit, has_loss),
            out_shape=(half, own) if section else (own,),
            in_specs=[smem] + [vmem] * (4 + len(extra)),
            out_specs=(vmem,) * (2 if section else 1),
            scratch_shapes=[pads],
            compiler_params=params,
        )(where, carried, preact_of[section], weights, grads, *extra)
        carried = carried[0] if section else None
    summed_ring.finish()
    grads, summed_ring.blocks, taps_from = lax.optimization_barrier((grads, summed_ring.blocks, taps_from))

    ring = Ring(grads.reshape(rows, own_cols, chans))
    ring.step()

    chunk = min(rows, 8)
    grid_shape = pltpu.VMEM((tiles, rows + 2, strips, own_cols, chans), jnp.bfloat16)
    pieces = max(-(-(g * share % chans + share) // chans) for g in range(groups))
    params = pltpu.CompilerParams(vmem_limit_bytes=(16 << 20) + 8 * groups * rows * own_cols * chans)
    columns = pl.pallas_call(
        functools.partial(columns_kernel, rows, strips, chunk),
        out_shape=jax.ShapeDtypeStruct((tiles, rows // chunk, share, chunk * BAND_COLS), jnp.bfloat16),
        in_specs=[smem] * 2 + [vmem] * len(summed_ring.blocks),
        out_specs=vmem,
        scratch_shapes=[
            grid_shape,
            pltpu.VMEM((3, (chunk + 2) * BAND_COLS, chans), jnp.float32),
            pltpu.VMEM((pieces * chans, chunk * BAND_COLS), jnp.float32),
        ],
        compiler_params=params,
    )(sources, spot, *summed_ring.blocks)

    while ring.done < ring.steps - 2:
        ring.step()
    arrived = list(ring.blocks)
    columns = ring.after(columns)
    ring.step()
    chunk_shape = pltpu.VMEM((3, (chunk + 2) * BAND_COLS, chans), jnp.bfloat16)

    def convolve_tile(which):
        return pl.pallas_call(
            functools.partial(early_gradient_kernel, rows, strips, chunk, which),
            out_shape=jax.ShapeDtypeStruct((rows, BAND_COLS, chans), jnp.bfloat16),
            in_specs=[smem] * 2 + [vmem] * (1 + len(arrived)),
            out_specs=vmem,
            scratch_shapes=[grid_shape, chunk_shape],
            compiler_params=params,
        )(sources, todo, weights, *arrived)

    inner = [convolve_tile(which) for which in range(tiles - 2)]
    inner[0] = ring.after(inner[0])
    ring.finish()
    conv_grad, lateral_grad = pl.pallas_call(
        functools.partial(late_gradient_kernel, rows, strips, chunk, sections, micros),
        out_shape=(
            jax.ShapeDtypeStruct((share, chans), jnp.float32),
            jax.ShapeDtypeStruct((depth, chans), jnp.float32),
        ),
        in_specs=[smem] * 3 + [vmem] * (2 + len(inner) + len(taps_from) + len(ring.blocks)),
        out_specs=(vmem, vmem),
        scratch_shapes=[
            grid_shape,
            chunk_shape,
            pltpu.VMEM((tiles, rows, BAND_COLS, chans), jnp.bfloat16),
            pltpu.VMEM((sections * micros * local, chans), jnp.bfloat16),
        ],
        compiler_params=params,
    )(sources, todo, mine, weights, columns, *inner, *taps_from, *ring.blocks)
    return (conv_grad[None], lateral_grad[None])


def solution(mesh):
    placed = (
        P(None, None, ("dp", "section"), None),
        P("section", "dp", None),
        P("section", None, None),
        P(),
        P("dp", None),
        P(None, "dp"),
    )
    return jax.shard_map(
        on_device,
        mesh=mesh,
        in_specs=placed,
        out_specs=(P("section", "dp", None), P("section", "dp", None)),
        check_vma=False,
    )
```
